768 devices in a mesh: dp: 24 (over z, core), ctx: 32 (over y, x).
Axes of the slice: x: 4, y: 8, z: 12, core: 2. Of those that a mesh axis runs over, the one named last changes fastest.
Arguments:
- queries: bfloat16 [122880, 2048], P(('dp', 'ctx')), may hold values from -10 to 10
- key_value: bfloat16 [12288, 2, 2048], P(('dp', 'ctx')), may hold values from -10 to 10
- out_grad: bfloat16 [122880, 2048], P(('dp', 'ctx')), may hold values from -6 to 6
- packing: int32 [12288], P(('dp', 'ctx')), may hold values from 0 to 383, as said below
- memory_docs: int32 [24, 512], P('dp'), may hold values from 0 to 15, never falling along the last dimension, each value on 1 to 170 neighbouring positions
- decoder_docs: int32 [24, 5120], P('dp', 'ctx'), may hold values from 0 to 15, never falling along the last dimension, each value on 1 to 1706 neighbouring positions
Outputs:
- attended: bfloat16 [122880, 2048], P(('dp', 'ctx'))
- query_grad: bfloat16 [122880, 2048], P(('dp', 'ctx'))
- key_value_grad: bfloat16 [12288, 2, 2048], P(('dp', 'ctx'))
The draws below stay inside these ranges and needn't reach their ends.
Inputs may be any that keep to these rules, and one draw needn't show every extreme that they name: For each ctx index c, packing maps the 384 encoder tokens of ctx index c one to one onto 0 .. 383; packing // 16 is the token's group. No device sends more than 2 tokens to one group, and every device sends exactly 2 tokens to at least one group. `memory_docs`: within a group, document ids never fall along the memory rows, every id 0 .. 15 occurs, a document has at most 170 memory rows, and one has exactly that many. `decoder_docs`: within a group, document ids never fall along the decoder rows, every id 0 .. 15 occurs, a document has at most 1706 decoder rows, and one has exactly that many.
All inputs are finite; a program needn't handle non-finite values.
Results may differ from the reference program's by a relative error of at most 0.014.
The reference program's roundings to bfloat16 on the way count: a program that leaves them out, or rounds other values in their place, can miss the bound.
Values may be sent and summed in bfloat16 or wider, within the bound.
No kernel may reach another device: no remote copies, remote signals or barrier semaphores. Data moves between devices by JAX's collectives and lax.ppermute only.
A program may use at most 64 MiB of HBM per device.

```python
import math
import jax
import jax.numpy as jnp
import numpy as np
from jax import lax

HEADS = 32
DH = 64
E_DEV = 16
Q_DEV = 160
CAP = 2
K_G = 512
Q_G = 5120
NDOC = 16
MEM_MOST = 170
DEC_MOST = 1706
ENC = 12288
DEC = 122880
N_DP = 24
N_CTX = 32


def draw_queries(key, part):
    key = jax.random.fold_in(key, 21)
    first_key = jax.random.fold_in(key, 0)
    values = jax.random.normal(first_key, (DEC, HEADS * DH), jnp.float32)
    return jnp.clip(values, -10.0, 10.0).astype(jnp.bfloat16)


def draw_key_value(key, part):
    key = jax.random.fold_in(key, 22)
    first_key = jax.random.fold_in(key, 0)
    values = jax.random.normal(first_key, (ENC, 2, HEADS * DH), jnp.float32)
    return jnp.clip(values, -10.0, 10.0).astype(jnp.bfloat16)


def draw_packing(key, part):
    key = jax.random.fold_in(key, 11)

    def one_column(column_key):
        keys = jax.random.split(column_key, 6)
        multiset = jnp.arange(CAP * N_DP, dtype=jnp.int32) % N_DP
        chosen_value = jax.random.randint(keys[0], (), 0, N_DP)
        ranking = jax.random.permutation(keys[1], CAP * N_DP).astype(jnp.int32)
        ranking = jnp.where(multiset == chosen_value, ranking - CAP * N_DP, ranking)
        ordering = jnp.argsort(ranking, stable=True)
        picked = multiset[ordering][:E_DEV]
        shifts = jax.random.permutation(keys[2], N_DP).astype(jnp.int32)
        relabel = jax.random.permutation(keys[3], N_DP).astype(jnp.int32)
        token_keys = jax.random.split(keys[4], N_DP)
        orders = jax.vmap(lambda one_key: jax.random.permutation(one_key, E_DEV))(token_keys)
        sigma = picked[orders]
        target_group = relabel[(shifts[:, None] + sigma) % N_DP].reshape(-1)
        row_scores = jax.random.permutation(keys[5], N_DP * E_DEV).astype(jnp.int32)
        same_group = target_group[:, None] == target_group[None, :]
        below = row_scores[None, :] < row_scores[:, None]
        memory_row = jnp.sum(same_group & below, axis=1).astype(jnp.int32)
        return target_group * E_DEV + memory_row
    columns = jax.vmap(one_column)(jax.random.split(key, N_CTX))
    return columns.reshape(N_CTX, N_DP, E_DEV).transpose(1, 0, 2).reshape(-1).astype(jnp.int32)


def steps_of(stream_key, shape, cuts, least, largest):
    factor_of, own = 1.0, jax.random.fold_in(stream_key, 6)
    for position, shards_of in cuts:
        steps = jnp.exp(jax.random.uniform(jax.random.fold_in(own, position), (shards_of,), jnp.float32, least / len(cuts), largest / len(cuts)))
        factor_of = factor_of * jnp.repeat(steps, shape[position] // shards_of).reshape([-1 if axis == position else 1 for axis in range(len(shape))])
    return factor_of


def profile(count, total, bound, lean):
    weights = [(1 << 20) // math.isqrt(grade ** lean) + 1 for grade in range(2, count + 1)]
    rest, holding = total - bound - (count - 1), [1] * (count - 1)
    while rest > 0:
        movable = [i for i in range(count - 1) if holding[i] < bound]
        mass, remaining = sum([weights[i] for i in movable]), rest
        for i in movable:
            more = min(bound - holding[i], max(1, remaining * weights[i] // mass), rest)
            holding[i] = holding[i] + more
            rest = rest - more
    return np.array([bound] + holding)


def uneven(stream_key, count, total, most, lean):
    if count == 2:
        one = jax.random.randint(stream_key, (), max(1, total - most), min(most, total - 1) + 1)
        return jnp.stack([one, total - one])
    lengths = jnp.asarray(profile(count, total, most, lean), jnp.int32)
    twos = (count - 1) // 2
    giver, taker = lengths[1:1 + 2 * twos:2], lengths[2:2 + 2 * twos:2]
    margin = jnp.minimum(giver - 1, most - taker)
    passed = jax.random.randint(jax.random.fold_in(stream_key, 1), (twos,), 0, 1 << 20) % (margin + 1)
    lengths = lengths.at[1:1 + 2 * twos:2].set(giver - passed).at[2:2 + 2 * twos:2].set(taker + passed)
    return lengths[jax.random.permutation(jax.random.fold_in(stream_key, 2), count)]


def bell_draw(own_key, shape, deviation, most, shards=(), held_as=jnp.bfloat16):
    gain = steps_of(own_key, shape, shards, -0.22, 0.18) if shards else 1.0
    result = jax.random.normal(own_key, shape, jnp.float32) * deviation * gain
    return jnp.minimum(jnp.maximum(result, -most), most).astype(held_as)


def setup_inputs(seed: int = 0) -> dict:
    arg_keys = jax.random.split(jax.random.key(seed), 7)
    return {
        "queries": draw_queries(jax.random.fold_in(arg_keys[6], 71), 0),
        "key_value": draw_key_value(jax.random.fold_in(arg_keys[6], 71), 0),
        "out_grad": bell_draw(arg_keys[2], (DEC, HEADS * DH), 1.0, 6.0, ((0, 768),)),
        "packing": draw_packing(jax.random.fold_in(arg_keys[6], 71), 0),
        "memory_docs": jax.vmap(lambda own: jnp.searchsorted(jnp.cumsum(uneven(own, NDOC, K_G, MEM_MOST, 2)), jnp.arange(K_G), side="right"))(jax.random.split(arg_keys[4], N_DP)).reshape((N_DP, K_G)).astype(jnp.int32),
        "decoder_docs": jax.vmap(lambda own: jnp.searchsorted(jnp.cumsum(uneven(own, NDOC, Q_G, DEC_MOST, 2)), jnp.arange(Q_G), side="right"))(jax.random.split(arg_keys[5], N_DP)).reshape((N_DP, Q_G)).astype(jnp.int32),
    }


MASKED = -1e+30

def attend_device(queries_dev, grads_dev, docs_dev, memory_group, docs_group):
    width_all = queries_dev.shape[1]
    heads_count = width_all // DH
    score_scale = 1.0 / math.sqrt(DH)
    highest = lax.Precision.HIGHEST
    query_heads = queries_dev.astype(jnp.float32).reshape(-1, heads_count, DH)
    grad_heads = grads_dev.astype(jnp.float32).reshape(-1, heads_count, DH)
    key_heads = memory_group[:, :width_all].astype(jnp.float32).reshape(-1, heads_count, DH)
    value_heads = memory_group[:, width_all:].astype(jnp.float32).reshape(-1, heads_count, DH)
    allowed = docs_dev[:, None] == docs_group[None, :]
    scores = jnp.einsum('qhd,khd->hqk', query_heads, key_heads, precision=highest) * score_scale
    scores = jnp.where(allowed[None], scores, MASKED)
    row_max = lax.optimization_barrier(jnp.max(scores, axis=-1, keepdims=True))
    weights = jnp.where(allowed[None], jnp.exp(scores - row_max), 0.0)
    normed = weights / lax.optimization_barrier(jnp.sum(weights, axis=-1, keepdims=True))
    rounded = lax.optimization_barrier(normed.astype(jnp.bfloat16)).astype(jnp.float32)
    attended = jnp.einsum('hqk,khd->qhd', rounded, value_heads, precision=highest)
    grad_normed = jnp.einsum('qhd,khd->hqk', grad_heads, value_heads, precision=highest)
    row_delta = lax.optimization_barrier(jnp.sum(normed * grad_normed, axis=-1, keepdims=True))
    grad_scores = (normed * (grad_normed - row_delta)).astype(jnp.bfloat16)
    grad_scores = lax.optimization_barrier(grad_scores).astype(jnp.float32)
    query_grad = jnp.einsum('hqk,khd->qhd', grad_scores, key_heads, precision=highest) * score_scale
    key_grad = jnp.einsum('hqk,qhd->khd', grad_scores, query_heads, precision=highest) * score_scale
    value_grad = jnp.einsum('hqk,qhd->khd', rounded, grad_heads, precision=highest)
    row_count = queries_dev.shape[0]
    key_term = jnp.concatenate([key_grad.reshape(-1, width_all), value_grad.reshape(-1, width_all)], axis=1)
    return (attended.reshape(row_count, width_all).astype(jnp.bfloat16), query_grad.reshape(row_count, width_all).astype(jnp.bfloat16), key_term)

def reference(queries, key_value, out_grad, packing, memory_docs, decoder_docs):
    width_all = HEADS * DH
    token_index = jnp.arange(ENC, dtype=jnp.int32)
    column = token_index // E_DEV % N_CTX
    target = (packing // E_DEV * N_CTX + column) * E_DEV + packing % E_DEV
    flat_pairs = key_value.reshape(ENC, 2 * width_all)
    memory = jnp.zeros((ENC, 2 * width_all), jnp.bfloat16).at[target].set(flat_pairs)
    memory = memory.reshape(N_DP, K_G, 2 * width_all)
    query_groups = queries.reshape(N_DP, N_CTX, Q_DEV, width_all)
    grad_groups = out_grad.reshape(N_DP, N_CTX, Q_DEV, width_all)
    doc_groups = decoder_docs.reshape(N_DP, N_CTX, Q_DEV)

    def one_group(inputs):
        memory_group, docs_group, query_devs, grad_devs, doc_devs = inputs

        def one_device(running, pieces):
            attended, query_grad, key_term = attend_device(pieces[0], pieces[1], pieces[2], memory_group, docs_group)
            rounded_term = lax.optimization_barrier(key_term.astype(jnp.bfloat16)).astype(jnp.float32)
            return (running + rounded_term, (attended, query_grad))
        running, outputs = lax.scan(one_device, jnp.zeros((K_G, 2 * width_all), jnp.float32), (query_devs, grad_devs, doc_devs))
        return (outputs[0], outputs[1], running.astype(jnp.bfloat16))
    attended, query_grad, memory_grad = lax.map(one_group, (memory, memory_docs, query_groups, grad_groups, doc_groups))
    key_value_grad = memory_grad.reshape(ENC, 2 * width_all)[target].reshape(ENC, 2, width_all)
    return (attended.reshape(DEC, width_all), query_grad.reshape(DEC, width_all), key_value_grad)
```

```python
import functools
import math

import jax
import jax.numpy as jnp
from jax import lax
from jax.experimental import pallas as pl
from jax.experimental.pallas import tpu as pltpu
from jax.sharding import PartitionSpec as P

DH = 64
LANES = 128
FAR = -1e30
BLOCK = 4
VMEM_BYTES = 48 * 1024 * 1024
ANY = pl.BlockSpec(memory_space=pl.ANY)
SMEM = pl.BlockSpec(memory_space=pltpu.SMEM)


def run_copies(copies):
    for copy in copies:
        copy.start()
    for copy in copies:
        copy.wait()


def pack_kernel(member_ref, queries_ref, grads_ref, docs_ref, *rest):
    pieces, sems = rest[:-1], rest[-1]
    half = queries_ref.shape[1] // len(pieces)
    copies = []
    for d, piece in enumerate(pieces):
        columns = pl.ds(pl.multiple_of((member_ref[0] ^ d) * half, half), half)
        copies += [
            pltpu.make_async_copy(
                queries_ref.at[:, columns], piece.at[:, pl.ds(0, half)], sems.at[d, 0]
            ),
            pltpu.make_async_copy(
                grads_ref.at[:, columns], piece.at[:, pl.ds(half, half)], sems.at[d, 1]
            ),
            pltpu.make_async_copy(docs_ref, piece.at[:, pl.ds(2 * half, LANES)], sems.at[d, 2]),
        ]
    run_copies(copies)


def pack(member, queries, grads, docs):
    rows, width = queries.shape
    piece = jax.ShapeDtypeStruct((rows, 2 * width // BLOCK + LANES), queries.dtype)
    return pl.pallas_call(
        pack_kernel,
        out_shape=[piece] * BLOCK,
        in_specs=[SMEM, ANY, ANY, ANY],
        out_specs=[ANY] * BLOCK,
        scratch_shapes=[pltpu.SemaphoreType.DMA((BLOCK, 3))],
        cost_estimate=pl.CostEstimate(
            flops=0, bytes_accessed=4 * 2 * rows * width, transcendentals=0
        ),
        name="pack",
    )(member, queries, grads, docs)


def unpack_kernel(member_ref, *rest):
    pieces, (attended_ref, query_grad_ref, sems) = rest[:-3], rest[-3:]
    half = attended_ref.shape[1] // len(pieces)
    copies = []
    for d, piece in enumerate(pieces):
        columns = pl.ds(pl.multiple_of((member_ref[0] ^ d) * half, half), half)
        for which, out_ref in enumerate((attended_ref, query_grad_ref)):
            copies.append(
                pltpu.make_async_copy(
                    piece.at[:, pl.ds(which * half, half)],
                    out_ref.at[:, columns],
                    sems.at[d, which],
                )
            )
    run_copies(copies)


def unpack(member, pieces, width):
    rows = pieces[0].shape[0]
    out = jax.ShapeDtypeStruct((rows, width), pieces[0].dtype)
    return pl.pallas_call(
        unpack_kernel,
        out_shape=[out, out],
        in_specs=[SMEM] + [ANY] * BLOCK,
        out_specs=[ANY, ANY],
        scratch_shapes=[pltpu.SemaphoreType.DMA((BLOCK, 2))],
        cost_estimate=pl.CostEstimate(
            flops=0, bytes_accessed=4 * 2 * rows * width, transcendentals=0
        ),
        name="unpack",
    )(member, *pieces)


def nt_dot(left, right):
    return lax.dot_general(
        left, right, (((1,), (1,)), ((), ())), preferred_element_type=jnp.float32
    )


def tn_dot(left, right):
    return lax.dot_general(
        left, right, (((0,), (0,)), ((), ())), preferred_element_type=jnp.float32
    )


def nn_dot(left, right):
    return jnp.dot(left, right, preferred_element_type=jnp.float32)


def attend_kernel(far_ref, kv_ref, *rest):
    pieces, rest = rest[:BLOCK], rest[BLOCK:]
    grad_ref, outs, rest = rest[0], rest[1 : 1 + BLOCK], rest[1 + BLOCK :]
    held, keys, values, rounded, grad_scores, result, sems = rest
    rows = pieces[0].shape[0]
    mem_rows, width = kv_ref.shape
    half = width // 2
    scale = 1.0 / math.sqrt(DH)
    loads = [
        pltpu.make_async_copy(piece, held.at[pl.ds(d * rows, rows)], sems.at[d])
        for d, piece in enumerate(pieces)
    ]
    run_copies(loads)
    low = lax.broadcasted_iota(jnp.int32, (mem_rows, LANES), 1) < DH
    zero = jnp.zeros((mem_rows, LANES), jnp.bfloat16)
    keys[pl.ds(0, mem_rows), pl.ds(LANES, LANES)] = far_ref[...]
    keys[pl.ds(mem_rows, mem_rows), pl.ds(LANES, LANES)] = far_ref[...]
    for pair in range(half // LANES):
        key_columns = pl.ds(pair * LANES, LANES)
        value_columns = pl.ds(half + pair * LANES, LANES)
        key_pair = kv_ref[:, key_columns] * jnp.bfloat16(scale)
        value_pair = kv_ref[:, value_columns]
        keys[pl.ds(0, mem_rows), pl.ds(0, LANES)] = jnp.where(low, key_pair, zero)
        keys[pl.ds(mem_rows, mem_rows), pl.ds(0, LANES)] = jnp.where(low, zero, key_pair)
        values[pl.ds(0, mem_rows)] = jnp.where(low, value_pair, zero)
        values[pl.ds(mem_rows, mem_rows)] = jnp.where(low, zero, value_pair)

        def step(index, carry):
            here = pl.ds(pl.multiple_of(index * rows, rows), rows)
            query = jnp.concatenate([held[here, key_columns], held[here, pl.ds(width, LANES)]], 1)
            scores = nt_dot(query, keys[...])
            grad_normed = nt_dot(held[here, value_columns], values[...])
            for head in range(2):
                mine = slice(head * mem_rows, (head + 1) * mem_rows)
                part = scores[:, mine]
                weights = jnp.exp(part - jnp.max(part, axis=1, keepdims=True))
                normed = weights * (1.0 / jnp.sum(weights, axis=1, keepdims=True))
                part_grad = grad_normed[:, mine]
                delta = jnp.sum(normed * part_grad, axis=1, keepdims=True)
                rounded[here, mine] = normed.astype(jnp.bfloat16)
                grad_scores[here, mine] = (normed * (part_grad - delta)).astype(jnp.bfloat16)
            result[here, key_columns] = nn_dot(rounded[here, :], values[...]).astype(jnp.bfloat16)
            result[here, value_columns] = nn_dot(
                grad_scores[here, :], keys[:, pl.ds(0, LANES)]
            ).astype(jnp.bfloat16)
            return carry

        lax.fori_loop(0, BLOCK, step, 0)
        key_grad = tn_dot(grad_scores[...], held[:, key_columns]) * scale
        value_grad = tn_dot(rounded[...], held[:, value_columns])
        grad_ref[:, key_columns] = jnp.where(
            low, key_grad[:mem_rows], key_grad[mem_rows:]
        ).astype(jnp.bfloat16)
        grad_ref[:, value_columns] = jnp.where(
            low, value_grad[:mem_rows], value_grad[mem_rows:]
        ).astype(jnp.bfloat16)
    run_copies(
        [
            pltpu.make_async_copy(result.at[pl.ds(d * rows, rows)], out, sems.at[d])
            for d, out in enumerate(outs)
        ]
    )


def attend(far, memory, pieces):
    rows = pieces[0].shape[0]
    mem_rows, width = memory.shape
    all_rows = BLOCK * rows
    half = jnp.bfloat16
    return pl.pallas_call(
        attend_kernel,
        out_shape=[jax.ShapeDtypeStruct((mem_rows, width), half)]
        + [jax.ShapeDtypeStruct((rows, width), half)] * BLOCK,
        in_specs=[pl.BlockSpec(memory_space=pltpu.VMEM)] * 2 + [ANY] * BLOCK,
        out_specs=[pl.BlockSpec(memory_space=pltpu.VMEM)] + [ANY] * BLOCK,
        scratch_shapes=[
            pltpu.VMEM((all_rows, width + LANES), half),
            pltpu.VMEM((2 * mem_rows, 2 * LANES), half),
            pltpu.VMEM((2 * mem_rows, LANES), half),
            pltpu.VMEM((all_rows, 2 * mem_rows), half),
            pltpu.VMEM((all_rows, 2 * mem_rows), half),
            pltpu.VMEM((all_rows, width), half),
            pltpu.SemaphoreType.DMA((BLOCK,)),
        ],
        compiler_params=pltpu.CompilerParams(vmem_limit_bytes=VMEM_BYTES),
        cost_estimate=pl.CostEstimate(
            flops=6 * 2 * all_rows * mem_rows * width // 2,
            bytes_accessed=8 * all_rows * width,
            transcendentals=all_rows * mem_rows * width // (2 * DH),
        ),
        name="attend",
    )(far, memory, *pieces)


def shards(queries, key_value, out_grad, packing, memory_docs, decoder_docs):
    group_count = lax.axis_size("dp")
    column_count = lax.axis_size("ctx")
    enc_rows, _, head_width = key_value.shape
    part_width = 2 * head_width // BLOCK
    slot_cap = 2
    slot_count = group_count * slot_cap
    half = jnp.bfloat16

    target_group = packing // enc_rows
    token_index = jnp.arange(enc_rows, dtype=jnp.int32)
    earlier = (target_group[:, None] == target_group[None, :]) & (
        token_index[None, :] < token_index[:, None]
    )
    send_slot = target_group * slot_cap + jnp.sum(earlier, axis=1)
    placing = jnp.arange(slot_count, dtype=jnp.int32)[:, None] == send_slot[None, :]
    placing_half = placing.astype(half)
    labels = jnp.broadcast_to(
        (packing % enc_rows + 1).astype(half)[:, None], (enc_rows, LANES)
    )
    flat_pairs = jnp.concatenate([key_value.reshape(enc_rows, 2 * head_width), labels], axis=1)
    send_pairs = jnp.dot(placing_half, flat_pairs, preferred_element_type=jnp.float32).astype(half)
    received = lax.all_to_all(send_pairs, "dp", split_axis=0, concat_axis=0, tiled=True)

    member = lax.axis_index("ctx") % BLOCK
    member_ref = member.reshape(1).astype(jnp.int32)
    doc_lanes = jnp.arange(LANES, dtype=jnp.int32)
    row_docs = (decoder_docs[0][:, None] == doc_lanes[None, :]).astype(half)
    far = jnp.where(memory_docs[0][:, None] == doc_lanes[None, :], 0.0, FAR).astype(half)
    pieces = pack(member_ref, queries, out_grad, row_docs)
    exchange = [
        [(c, c ^ d) for c in range(column_count)] for d in range(BLOCK)
    ]
    pieces = [pieces[0]] + [
        lax.ppermute(pieces[d], "ctx", exchange[d]) for d in range(1, BLOCK)
    ]

    recv_label = received[:, 2 * head_width].astype(jnp.int32)
    filling = recv_label[:, None] - 1 == token_index[None, :]
    filling_half = filling.astype(half)
    memory = jnp.dot(
        filling_half.T, received[:, : 2 * head_width], preferred_element_type=jnp.float32
    ).astype(half)
    by_member = memory.reshape(enc_rows, 2, BLOCK, part_width // 2).transpose(2, 0, 1, 3)
    by_member = by_member.reshape(1, BLOCK, enc_rows, part_width)
    by_column = jnp.broadcast_to(
        by_member, (column_count // BLOCK, BLOCK, enc_rows, part_width)
    ).reshape(column_count, enc_rows, part_width)
    group_part = lax.all_to_all(by_column, "ctx", split_axis=0, concat_axis=0, tiled=True)
    group_part = group_part.reshape(column_count * enc_rows, part_width)

    part_grad, *results = attend(far, group_part, pieces)

    part_grad = part_grad.reshape(column_count, enc_rows, part_width)
    partials = lax.all_to_all(part_grad, "ctx", split_axis=0, concat_axis=0, tiled=True)
    partials = partials.reshape(column_count // BLOCK, BLOCK, enc_rows, 2, part_width // 2)
    memory_grad = jnp.sum(partials.astype(jnp.float32), axis=0).astype(half)
    memory_grad = memory_grad.transpose(1, 2, 0, 3).reshape(enc_rows, 2 * head_width)
    back_pairs = jnp.dot(filling_half, memory_grad, preferred_element_type=jnp.float32).astype(half)
    returned = lax.all_to_all(back_pairs, "dp", split_axis=0, concat_axis=0, tiled=True)
    enc_grads = jnp.dot(placing_half.T, returned, preferred_element_type=jnp.float32).astype(half)

    results = [results[0]] + [
        lax.ppermute(results[d], "ctx", exchange[d]) for d in range(1, BLOCK)
    ]
    attended, query_grad = unpack(member_ref, results, head_width)
    return attended, query_grad, enc_grads.reshape(enc_rows, 2, head_width)


def solution(mesh):
    return jax.shard_map(
        shards,
        mesh=mesh,
        in_specs=(
            P(("dp", "ctx"), None),
            P(("dp", "ctx"), None, None),
            P(("dp", "ctx"), None),
            P(("dp", "ctx")),
            P("dp", None),
            P("dp", "ctx"),
        ),
        out_specs=(P(("dp", "ctx"), None), P(("dp", "ctx"), None), P(("dp", "ctx"), None, None)),
        check_vma=False,
    )
```

```python
import math

import jax
import jax.numpy as jnp
from jax import lax
from jax.experimental import pallas as pl
from jax.experimental.pallas import tpu as pltpu
from jax.sharding import PartitionSpec as P

DH = 64
LANES = 128
FAR = -1e30
BLOCK = 8
CHUNK = 256
SPANS = (128, 256, 512)
VMEM_BYTES = 48 * 1024 * 1024
COPY_BYTES = 16 * 1024 * 1024
EARLY = 4
RETURNED = 4
VMEM = pl.BlockSpec(memory_space=pltpu.VMEM)
ANY = pl.BlockSpec(memory_space=pl.ANY)
SMEM = pl.BlockSpec(memory_space=pltpu.SMEM)


def run_copies(copies):
    for copy in copies:
        copy.start()
    for copy in copies:
        copy.wait()


def pack_kernel(member_ref, queries_ref, grads_ref, docs_ref, *pieces):
    half = queries_ref.shape[1] // len(pieces)
    for d, piece in enumerate(pieces):
        columns = pl.ds(pl.multiple_of((member_ref[0] ^ d) * half, half), half)
        piece[:, pl.ds(0, half)] = queries_ref[:, columns]
        piece[:, pl.ds(half, half)] = grads_ref[:, columns]
        piece[:, pl.ds(2 * half, LANES)] = docs_ref[...]


def pack(member, queries, grads, docs):
    rows, width = queries.shape
    piece = jax.ShapeDtypeStruct((rows, 2 * width // BLOCK + LANES), queries.dtype)
    return pl.pallas_call(
        pack_kernel,
        out_shape=[piece] * BLOCK,
        in_specs=[SMEM, VMEM, VMEM, VMEM],
        out_specs=[VMEM] * BLOCK,
        compiler_params=pltpu.CompilerParams(vmem_limit_bytes=COPY_BYTES),
        cost_estimate=pl.CostEstimate(
            flops=0, bytes_accessed=4 * 2 * rows * width, transcendentals=0
        ),
        name="pack",
    )(member, queries, grads, docs)


def unpack_kernel(member_ref, *rest):
    pieces, (attended_ref, query_grad_ref) = rest[:-2], rest[-2:]
    half = attended_ref.shape[1] // len(pieces)
    for d, piece in enumerate(pieces):
        columns = pl.ds(pl.multiple_of((member_ref[0] ^ d) * half, half), half)
        attended_ref[:, columns] = piece[:, pl.ds(0, half)]
        query_grad_ref[:, columns] = piece[:, pl.ds(half, half)]


def unpack(member, pieces, width):
    rows = pieces[0].shape[0]
    out = jax.ShapeDtypeStruct((rows, width), pieces[0].dtype)
    return pl.pallas_call(
        unpack_kernel,
        out_shape=[out, out],
        in_specs=[SMEM] + [VMEM] * BLOCK,
        out_specs=[VMEM, VMEM],
        compiler_params=pltpu.CompilerParams(vmem_limit_bytes=COPY_BYTES),
        cost_estimate=pl.CostEstimate(
            flops=0, bytes_accessed=4 * 2 * rows * width, transcendentals=0
        ),
        name="unpack",
    )(member, *pieces)


def nt_dot(left, right):
    return lax.dot_general(
        left, right, (((1,), (1,)), ((), ())), preferred_element_type=jnp.float32
    )


def tn_dot(left, right):
    return lax.dot_general(
        left, right, (((0,), (0,)), ((), ())), preferred_element_type=jnp.float32
    )


def nn_dot(left, right):
    return jnp.dot(left, right, preferred_element_type=jnp.float32)


def attend_kernel(member_ref, far_ref, spans_ref, kv_ref, *rest):
    pieces, rest = rest[:BLOCK], rest[BLOCK:]
    grad_ref, outs, rest = rest[0], rest[1 : 1 + BLOCK], rest[1 + BLOCK :]
    held, keys, key_aug, values, key_acc, value_acc, result, window, sems = rest
    rows = pieces[0].shape[0]
    mem_rows, width = kv_ref.shape
    half = width // 2
    pairs = half // LANES
    chunks = BLOCK * rows // CHUNK
    scale = 1.0 / math.sqrt(DH)

    def place(d):
        return pl.ds(pl.multiple_of((member_ref[0] ^ d) * rows, rows), rows)

    loads = [
        pltpu.make_async_copy(piece, held.at[place(d)], sems.at[d])
        for d, piece in enumerate(pieces)
    ]
    for load in loads:
        load.start()
    for load in loads:
        load.wait()
    for chunk in range(chunks):
        docs = held[pl.ds(chunk * CHUNK, CHUNK), pl.ds(width, LANES)].astype(jnp.float32)
        present = jnp.max(docs, axis=0, keepdims=True) > 0.0
        window[chunk, 0] = jnp.min(jnp.where(present, spans_ref[0:1], float(mem_rows))).astype(
            jnp.int32
        )
        window[chunk, 1] = jnp.max(jnp.where(present, spans_ref[1:2], 0.0)).astype(jnp.int32)
    low = lax.broadcasted_iota(jnp.int32, (mem_rows, LANES), 1) < DH
    zero = jnp.zeros((mem_rows, LANES), jnp.bfloat16)
    for pair in range(pairs):
        key_pair = kv_ref[:, pl.ds(pair * LANES, LANES)] * jnp.bfloat16(scale)
        value_pair = kv_ref[:, pl.ds(half + pair * LANES, LANES)]
        keys[pair] = key_pair
        for head in range(2):
            mine = low if head == 0 else ~low
            key_aug[pair, head, :, pl.ds(0, LANES)] = jnp.where(mine, key_pair, zero)
            key_aug[pair, head, :, pl.ds(LANES, LANES)] = far_ref[...]
            values[pair, head] = jnp.where(mine, value_pair, zero)
    key_acc[...] = jnp.zeros_like(key_acc)
    value_acc[...] = jnp.zeros_like(value_acc)

    def on_window(here, start, span):
        mine = pl.ds(start, span)
        docs = held[here, pl.ds(width, LANES)]
        half_lanes = lax.broadcasted_iota(jnp.int32, (span, LANES), 1) < DH
        key_columns = [pl.ds(pair * LANES, LANES) for pair in range(pairs)]
        value_columns = [pl.ds(half + pair * LANES, LANES) for pair in range(pairs)]
        query = [held[here, columns] for columns in key_columns]
        grad = [held[here, columns] for columns in value_columns]
        scores = [
            nt_dot(
                key_aug[pair, :, mine, :].reshape(2 * span, 2 * LANES),
                jnp.concatenate([query[pair], docs], axis=1),
            ).reshape(2, span, CHUNK)
            for pair in range(pairs)
        ]
        grad_normed = [
            nt_dot(values[pair, :, mine, :].reshape(2 * span, LANES), grad[pair]).reshape(
                2, span, CHUNK
            )
            for pair in range(pairs)
        ]
        rounded, grad_scores = [], []
        for pair in range(pairs):
            top = jnp.max(scores[pair], axis=1, keepdims=True)
            weights = jnp.exp(scores[pair] - top)
            normed = weights * (1.0 / jnp.sum(weights, axis=1, keepdims=True))
            delta = jnp.sum(normed * grad_normed[pair], axis=1, keepdims=True)
            rounded.append(normed.astype(jnp.bfloat16))
            grad_scores.append((normed * (grad_normed[pair] - delta)).astype(jnp.bfloat16))
        for pair in range(pairs):
            key_grad = nn_dot(grad_scores[pair].reshape(2 * span, CHUNK), query[pair])
            value_grad = nn_dot(rounded[pair].reshape(2 * span, CHUNK), grad[pair])
            key_acc[pair, mine, :] += jnp.where(half_lanes, key_grad[:span], key_grad[span:])
            value_acc[pair, mine, :] += jnp.where(half_lanes, value_grad[:span], value_grad[span:])
            key_turned = keys[pair, mine, :].T
            value_turned = kv_ref[mine, value_columns[pair]].T
            for columns, turned, terms in (
                (key_columns[pair], value_turned, rounded[pair]),
                (value_columns[pair], key_turned, grad_scores[pair]),
            ):
                both = [
                    nn_dot(turned[head * DH : (head + 1) * DH], terms[head]) for head in range(2)
                ]
                result[here, columns] = jnp.concatenate(both, axis=0).astype(jnp.bfloat16).T

    def step(chunk, carry):
        here = pl.ds(pl.multiple_of(chunk * CHUNK, CHUNK), CHUNK)
        first, last = window[chunk, 0], window[chunk, 1]
        taken = jnp.bool_(False)
        for span in SPANS:
            start = jnp.minimum((first // 16) * 16, mem_rows - span)
            fits = last <= start + span

            @pl.when(fits & ~taken)
            def _(start=start, span=span):
                on_window(here, pl.multiple_of(start, 16), span)

            taken = taken | fits
        return carry

    lax.fori_loop(0, chunks, step, 0)
    for pair in range(pairs):
        grad_ref[:, pl.ds(pair * LANES, LANES)] = (key_acc[pair] * scale).astype(jnp.bfloat16)
        grad_ref[:, pl.ds(half + pair * LANES, LANES)] = value_acc[pair].astype(jnp.bfloat16)
    run_copies(
        [
            pltpu.make_async_copy(result.at[place(d)], out, sems.at[d])
            for d, out in enumerate(outs)
        ]
    )


def attend(member, far, spans, memory, pieces):
    rows = pieces[0].shape[0]
    mem_rows, width = memory.shape
    all_rows = BLOCK * rows
    heads = width // (2 * DH)
    half = jnp.bfloat16
    return pl.pallas_call(
        attend_kernel,
        out_shape=[jax.ShapeDtypeStruct((mem_rows, width), half)]
        + [jax.ShapeDtypeStruct((rows, width), half)] * BLOCK,
        in_specs=[SMEM] + [VMEM] * 3 + [ANY] * BLOCK,
        out_specs=[VMEM] + [ANY] * BLOCK,
        scratch_shapes=[
            pltpu.VMEM((all_rows, width + LANES), half),
            pltpu.VMEM((heads // 2, mem_rows, LANES), half),
            pltpu.VMEM((heads // 2, 2, mem_rows, 2 * LANES), half),
            pltpu.VMEM((heads // 2, 2, mem_rows, LANES), half),
            pltpu.VMEM((heads // 2, mem_rows, LANES), jnp.float32),
            pltpu.VMEM((heads // 2, mem_rows, LANES), jnp.float32),
            pltpu.VMEM((all_rows, width), half),
            pltpu.SMEM((8, 2), jnp.int32),
            pltpu.SemaphoreType.DMA((BLOCK,)),
        ],
        compiler_params=pltpu.CompilerParams(vmem_limit_bytes=VMEM_BYTES),
        cost_estimate=pl.CostEstimate(
            flops=6 * 2 * all_rows * mem_rows * width // 2,
            bytes_accessed=8 * all_rows * width,
            transcendentals=all_rows * mem_rows * width // (2 * DH),
        ),
        name="attend",
    )(member, far, spans, memory, *pieces)


def shards(queries, key_value, out_grad, packing, memory_docs, decoder_docs):
    group_count = lax.axis_size("dp")
    column_count = lax.axis_size("ctx")
    enc_rows, _, head_width = key_value.shape
    part_width = 2 * head_width // BLOCK
    slot_cap = 2
    slot_count = group_count * slot_cap
    half = jnp.bfloat16

    target_group = packing // enc_rows
    token_index = jnp.arange(enc_rows, dtype=jnp.int32)
    earlier = (target_group[:, None] == target_group[None, :]) & (
        token_index[None, :] < token_index[:, None]
    )
    send_slot = target_group * slot_cap + jnp.sum(earlier, axis=1)
    placing = jnp.arange(slot_count, dtype=jnp.int32)[:, None] == send_slot[None, :]
    placing_half = placing.astype(half)
    labels = jnp.broadcast_to(
        (packing % enc_rows + 1).astype(half)[:, None], (enc_rows, LANES)
    )
    flat_pairs = jnp.concatenate([key_value.reshape(enc_rows, 2 * head_width), labels], axis=1)
    send_pairs = jnp.dot(placing_half, flat_pairs, preferred_element_type=jnp.float32).astype(half)
    received = lax.all_to_all(send_pairs, "dp", split_axis=0, concat_axis=0, tiled=True)

    member = lax.axis_index("ctx") % BLOCK
    member_ref = member.reshape(1).astype(jnp.int32)
    doc_lanes = jnp.arange(LANES, dtype=jnp.int32)
    row_docs = (decoder_docs[0][:, None] == doc_lanes[None, :]).astype(half)
    far = jnp.where(memory_docs[0][:, None] == doc_lanes[None, :], 0.0, FAR).astype(half)
    starts = jnp.sum(memory_docs[0][:, None] < doc_lanes[None, :], axis=0)
    ends = jnp.sum(memory_docs[0][:, None] <= doc_lanes[None, :], axis=0)
    spans = jnp.stack([starts, ends] + [starts] * 6).astype(jnp.float32)
    pieces = pack(member_ref, queries, out_grad, row_docs)
    exchange = [
        [(c, c ^ d) for c in range(column_count)] for d in range(BLOCK)
    ]
    pieces = [pieces[0]] + [
        lax.ppermute(pieces[d], "ctx", exchange[d]) for d in range(1, BLOCK)
    ]

    recv_label = received[:, 2 * head_width].astype(jnp.int32)
    filling = recv_label[:, None] - 1 == token_index[None, :]
    filling_half = filling.astype(half)
    memory = jnp.dot(
        filling_half.T, received[:, : 2 * head_width], preferred_element_type=jnp.float32
    ).astype(half)
    by_member = memory.reshape(enc_rows, 2, BLOCK, part_width // 2).transpose(2, 0, 1, 3)
    by_member = by_member.reshape(1, BLOCK, enc_rows, part_width)
    by_column = jnp.broadcast_to(
        by_member, (column_count // BLOCK, BLOCK, enc_rows, part_width)
    ).reshape(column_count, enc_rows, part_width)
    by_column, pieces[1 : 1 + EARLY] = lax.optimization_barrier(
        (by_column, pieces[1 : 1 + EARLY])
    )
    group_part = lax.all_to_all(by_column, "ctx", split_axis=0, concat_axis=0, tiled=True)
    group_part = group_part.reshape(column_count * enc_rows, part_width)

    part_grad, *results = attend(member_ref, far, spans, group_part, pieces)

    results = [results[0]] + [
        lax.ppermute(results[d], "ctx", exchange[d]) for d in range(1, BLOCK)
    ]
    part_grad = part_grad.reshape(column_count, enc_rows, part_width)
    partials = lax.all_to_all(part_grad, "ctx", split_axis=0, concat_axis=0, tiled=True)
    partials, results[1 : 1 + RETURNED] = lax.optimization_barrier(
        (partials, results[1 : 1 + RETURNED])
    )
    partials = partials.reshape(column_count // BLOCK, BLOCK, enc_rows, 2, part_width // 2)
    memory_grad = jnp.sum(partials.astype(jnp.float32), axis=0).astype(half)
    memory_grad = memory_grad.transpose(1, 2, 0, 3).reshape(enc_rows, 2 * head_width)
    back_pairs = jnp.dot(filling_half, memory_grad, preferred_element_type=jnp.float32).astype(half)
    returned = lax.all_to_all(back_pairs, "dp", split_axis=0, concat_axis=0, tiled=True)
    enc_grads = jnp.dot(placing_half.T, returned, preferred_element_type=jnp.float32).astype(half)

    attended, query_grad = unpack(member_ref, results, head_width)
    return attended, query_grad, enc_grads.reshape(enc_rows, 2, head_width)


def solution(mesh):
    return jax.shard_map(
        shards,
        mesh=mesh,
        in_specs=(
            P(("dp", "ctx"), None),
            P(("dp", "ctx"), None, None),
            P(("dp", "ctx"), None),
            P(("dp", "ctx")),
            P("dp", None),
            P("dp", "ctx"),
        ),
        out_specs=(P(("dp", "ctx"), None), P(("dp", "ctx"), None), P(("dp", "ctx"), None, None)),
        check_vma=False,
    )
```

```python
import math

import jax
import jax.numpy as jnp
from jax import lax
from jax.experimental import pallas as pl
from jax.experimental.pallas import tpu as pltpu
from jax.sharding import PartitionSpec as P

DH = 64
LANES = 128
TILE = 16
FAR = -1e30
BLOCK = 8
CHUNK = 256
SPANS = (64, 128, 256, 384, 512)
VMEM_BYTES = 48 * 1024 * 1024
COPY_BYTES = 16 * 1024 * 1024
EARLY, LATE = (2, 6, 5, 4), (7, 3, 1)
RETURNED, LAST = (2, 1, 3), (6, 7, 5, 4)
VMEM = pl.BlockSpec(memory_space=pltpu.VMEM)
ANY = pl.BlockSpec(memory_space=pl.ANY)
SMEM = pl.BlockSpec(memory_space=pltpu.SMEM)


def run_copies(copies):
    for copy in copies:
        copy.start()
    for copy in copies:
        copy.wait()


def pack_kernel(member_ref, queries_ref, grads_ref, bounds_ref, *pieces):
    half = queries_ref.shape[1] // len(pieces)
    rows = queries_ref.shape[0]
    for d, piece in enumerate(pieces):
        columns = pl.ds(pl.multiple_of((member_ref[0] ^ d) * half, half), half)
        piece[pl.ds(0, rows), pl.ds(0, half)] = queries_ref[:, columns]
        piece[pl.ds(0, rows), pl.ds(half, half)] = grads_ref[:, columns]
        piece[pl.ds(rows, TILE), :] = bounds_ref[...]


def pack(member, queries, grads, bounds):
    rows, width = queries.shape
    piece = jax.ShapeDtypeStruct((rows + TILE, 2 * width // BLOCK), queries.dtype)
    return pl.pallas_call(
        pack_kernel,
        out_shape=[piece] * BLOCK,
        in_specs=[SMEM, VMEM, VMEM, VMEM],
        out_specs=[VMEM] * BLOCK,
        compiler_params=pltpu.CompilerParams(vmem_limit_bytes=COPY_BYTES),
        cost_estimate=pl.CostEstimate(
            flops=0, bytes_accessed=4 * 2 * rows * width, transcendentals=0
        ),
        name="pack",
    )(member, queries, grads, bounds)


def unpack_kernel(member_ref, *rest):
    pieces, (attended_ref, query_grad_ref) = rest[:-2], rest[-2:]
    half = attended_ref.shape[1] // len(pieces)
    for d, piece in enumerate(pieces):
        columns = pl.ds(pl.multiple_of((member_ref[0] ^ d) * half, half), half)
        attended_ref[:, columns] = piece[:, pl.ds(0, half)]
        query_grad_ref[:, columns] = piece[:, pl.ds(half, half)]


def unpack(member, pieces, width):
    rows = pieces[0].shape[0]
    out = jax.ShapeDtypeStruct((rows, width), pieces[0].dtype)
    return pl.pallas_call(
        unpack_kernel,
        out_shape=[out, out],
        in_specs=[SMEM] + [VMEM] * BLOCK,
        out_specs=[VMEM, VMEM],
        compiler_params=pltpu.CompilerParams(vmem_limit_bytes=COPY_BYTES),
        cost_estimate=pl.CostEstimate(
            flops=0, bytes_accessed=4 * 2 * rows * width, transcendentals=0
        ),
        name="unpack",
    )(member, *pieces)


def nt_dot(left, right):
    return lax.dot_general(
        left, right, (((1,), (1,)), ((), ())), preferred_element_type=jnp.float32
    )


def tn_dot(left, right):
    return lax.dot_general(
        left, right, (((0,), (0,)), ((), ())), preferred_element_type=jnp.float32
    )


def nn_dot(left, right):
    return jnp.dot(left, right, preferred_element_type=jnp.float32)


def attend_kernel(member_ref, far_ref, spans_ref, kv_ref, *rest):
    pieces, rest = rest[:BLOCK], rest[BLOCK:]
    grad_ref, outs, rest = rest[0], rest[1 : 1 + BLOCK], rest[1 + BLOCK :]
    held, edges, spread, docs, keys, key_aug, values, key_acc, value_acc, result, window, sems = rest
    rows = pieces[0].shape[0] - TILE
    mem_rows, width = kv_ref.shape
    half = width // 2
    pairs = half // LANES
    chunks = BLOCK * rows // CHUNK
    scale = 1.0 / math.sqrt(DH)

    def place(d):
        return pl.ds(pl.multiple_of((member_ref[0] ^ d) * rows, rows), rows)

    loads = []
    for d, piece in enumerate(pieces):
        loads += [
            pltpu.make_async_copy(piece.at[pl.ds(0, rows)], held.at[place(d)], sems.at[0, d]),
            pltpu.make_async_copy(
                piece.at[pl.ds(rows, TILE), pl.ds(0, LANES)],
                edges.at[member_ref[0] ^ d],
                sems.at[1, d],
            ),
        ]
    for load in loads:
        load.start()
    low = lax.broadcasted_iota(jnp.int32, (mem_rows, LANES), 1) < DH
    zero = jnp.zeros((mem_rows, LANES), jnp.bfloat16)
    for pair in range(pairs):
        key_pair = kv_ref[:, pl.ds(pair * LANES, LANES)] * jnp.bfloat16(scale)
        value_pair = kv_ref[:, pl.ds(half + pair * LANES, LANES)]
        keys[pair] = key_pair
        for head in range(2):
            mine = low if head == 0 else ~low
            key_aug[pair, head, :, pl.ds(0, LANES)] = jnp.where(mine, key_pair, zero)
            key_aug[pair, head, :, pl.ds(LANES, LANES)] = far_ref[...]
            values[pair, head] = jnp.where(mine, value_pair, zero)
    key_acc[...] = jnp.zeros_like(key_acc)
    value_acc[...] = jnp.zeros_like(value_acc)

    for load in loads:
        load.wait()
    row = lax.broadcasted_iota(jnp.int32, (rows, LANES), 0).astype(jnp.float32)
    for source in range(BLOCK):
        edge = edges[source].astype(jnp.float32)
        first, last = edge[0:1], edge[1:2]
        inside = (row >= first) & (row < last)
        docs[pl.ds(source * rows, rows), :] = jnp.where(inside, 1.0, 0.0).astype(jnp.bfloat16)
        spread[0, pl.ds(source, 1), :] = first + source * rows
        spread[1, pl.ds(source, 1), :] = last + source * rows
    for chunk in range(chunks):
        opens = jnp.maximum(spread[0], float(chunk * CHUNK))
        present = opens < jnp.minimum(spread[1], float((chunk + 1) * CHUNK))
        window[chunk, 0] = jnp.min(jnp.where(present, spans_ref[0:1], float(mem_rows))).astype(
            jnp.int32
        )
        window[chunk, 1] = jnp.max(jnp.where(present, spans_ref[1:2], 0.0)).astype(jnp.int32)

    def on_window(here, start, span):
        mine = pl.ds(start, span)
        chunk_docs = docs[here, :]
        half_lanes = lax.broadcasted_iota(jnp.int32, (span, LANES), 1) < DH
        key_columns = [pl.ds(pair * LANES, LANES) for pair in range(pairs)]
        value_columns = [pl.ds(half + pair * LANES, LANES) for pair in range(pairs)]
        query = [held[here, columns] for columns in key_columns]
        grad = [held[here, columns] for columns in value_columns]
        scores = [
            nt_dot(
                key_aug[pair, :, mine, :].reshape(2 * span, 2 * LANES),
                jnp.concatenate([query[pair], chunk_docs], axis=1),
            ).reshape(2, span, CHUNK)
            for pair in range(pairs)
        ]
        grad_normed = [
            nt_dot(values[pair, :, mine, :].reshape(2 * span, LANES), grad[pair]).reshape(
                2, span, CHUNK
            )
            for pair in range(pairs)
        ]
        rounded, grad_scores = [], []
        for pair in range(pairs):
            top = jnp.max(scores[pair], axis=1, keepdims=True)
            weights = jnp.exp(scores[pair] - top)
            normed = weights * (1.0 / jnp.sum(weights, axis=1, keepdims=True))
            delta = jnp.sum(normed * grad_normed[pair], axis=1, keepdims=True)
            rounded.append(normed.astype(jnp.bfloat16))
            grad_scores.append((normed * (grad_normed[pair] - delta)).astype(jnp.bfloat16))
        for pair in range(pairs):
            key_grad = nn_dot(grad_scores[pair].reshape(2 * span, CHUNK), query[pair])
            value_grad = nn_dot(rounded[pair].reshape(2 * span, CHUNK), grad[pair])
            key_acc[pair, mine, :] += jnp.where(half_lanes, key_grad[:span], key_grad[span:])
            value_acc[pair, mine, :] += jnp.where(half_lanes, value_grad[:span], value_grad[span:])
            key_turned = keys[pair, mine, :].T
            value_turned = kv_ref[mine, value_columns[pair]].T
            for columns, turned, terms in (
                (key_columns[pair], value_turned, rounded[pair]),
                (value_columns[pair], key_turned, grad_scores[pair]),
            ):
                both = [
                    nn_dot(turned[head * DH : (head + 1) * DH], terms[head]) for head in range(2)
                ]
                result[here, columns] = jnp.concatenate(both, axis=0).astype(jnp.bfloat16).T

    def step(chunk, carry):
        here = pl.ds(pl.multiple_of(chunk * CHUNK, CHUNK), CHUNK)
        first, last = window[chunk, 0], window[chunk, 1]
        taken = jnp.bool_(False)
        for span in SPANS:
            start = jnp.minimum((first // 16) * 16, mem_rows - span)
            fits = last <= start + span

            @pl.when(fits & ~taken)
            def _(start=start, span=span):
                on_window(here, pl.multiple_of(start, 16), span)

            taken = taken | fits
        return carry

    lax.fori_loop(0, chunks, step, 0)
    for pair in range(pairs):
        grad_ref[:, pl.ds(pair * LANES, LANES)] = (key_acc[pair] * scale).astype(jnp.bfloat16)
        grad_ref[:, pl.ds(half + pair * LANES, LANES)] = value_acc[pair].astype(jnp.bfloat16)
    run_copies(
        [
            pltpu.make_async_copy(result.at[place(d)], out, sems.at[0, d])
            for d, out in enumerate(outs)
        ]
    )


def attend(member, far, spans, memory, pieces):
    rows = pieces[0].shape[0] - TILE
    mem_rows, width = memory.shape
    all_rows = BLOCK * rows
    heads = width // (2 * DH)
    half = jnp.bfloat16
    return pl.pallas_call(
        attend_kernel,
        out_shape=[jax.ShapeDtypeStruct((mem_rows, width), half)]
        + [jax.ShapeDtypeStruct((rows, width), half)] * BLOCK,
        in_specs=[SMEM] + [VMEM] * 3 + [ANY] * BLOCK,
        out_specs=[VMEM] + [ANY] * BLOCK,
        scratch_shapes=[
            pltpu.VMEM((all_rows, width), half),
            pltpu.VMEM((BLOCK, TILE, LANES), half),
            pltpu.VMEM((2, BLOCK, LANES), jnp.float32),
            pltpu.VMEM((all_rows, LANES), half),
            pltpu.VMEM((heads // 2, mem_rows, LANES), half),
            pltpu.VMEM((heads // 2, 2, mem_rows, 2 * LANES), half),
            pltpu.VMEM((heads // 2, 2, mem_rows, LANES), half),
            pltpu.VMEM((heads // 2, mem_rows, LANES), jnp.float32),
            pltpu.VMEM((heads // 2, mem_rows, LANES), jnp.float32),
            pltpu.VMEM((all_rows, width), half),
            pltpu.SMEM((8, 2), jnp.int32),
            pltpu.SemaphoreType.DMA((2, BLOCK)),
        ],
        compiler_params=pltpu.CompilerParams(vmem_limit_bytes=VMEM_BYTES),
        cost_estimate=pl.CostEstimate(
            flops=6 * 2 * all_rows * mem_rows * width // 2,
            bytes_accessed=8 * all_rows * width,
            transcendentals=all_rows * mem_rows * width // (2 * DH),
        ),
        name="attend",
    )(member, far, spans, memory, *pieces)


def shards(queries, key_value, out_grad, packing, memory_docs, decoder_docs):
    group_count = lax.axis_size("dp")
    column_count = lax.axis_size("ctx")
    enc_rows, _, head_width = key_value.shape
    part_width = 2 * head_width // BLOCK
    slot_cap = 2
    slot_count = group_count * slot_cap
    half = jnp.bfloat16

    target_group = packing // enc_rows
    token_index = jnp.arange(enc_rows, dtype=jnp.int32)
    earlier = (target_group[:, None] == target_group[None, :]) & (
        token_index[None, :] < token_index[:, None]
    )
    send_slot = target_group * slot_cap + jnp.sum(earlier, axis=1)
    placing = jnp.arange(slot_count, dtype=jnp.int32)[:, None] == send_slot[None, :]
    placing_half = placing.astype(half)
    labels = jnp.broadcast_to(
        (packing % enc_rows + 1).astype(half)[:, None], (enc_rows, LANES)
    )
    flat_pairs = jnp.concatenate([key_value.reshape(enc_rows, 2 * head_width), labels], axis=1)
    send_pairs = jnp.dot(placing_half, flat_pairs, preferred_element_type=jnp.float32).astype(half)
    received = lax.all_to_all(send_pairs, "dp", split_axis=0, concat_axis=0, tiled=True)

    member = lax.axis_index("ctx") % BLOCK
    member_ref = member.reshape(1).astype(jnp.int32)
    doc_lanes = jnp.arange(LANES, dtype=jnp.int32)
    bounds = jnp.stack(
        [
            jnp.sum(decoder_docs[0][:, None] < doc_lanes[None, :], axis=0),
            jnp.sum(decoder_docs[0][:, None] <= doc_lanes[None, :], axis=0),
        ]
    ).astype(half)
    bounds = jnp.pad(bounds, ((0, TILE - 2), (0, part_width - LANES)))
    far = jnp.where(memory_docs[0][:, None] == doc_lanes[None, :], 0.0, FAR).astype(half)
    starts = jnp.sum(memory_docs[0][:, None] < doc_lanes[None, :], axis=0)
    ends = jnp.sum(memory_docs[0][:, None] <= doc_lanes[None, :], axis=0)
    spans = jnp.stack([starts, ends] + [starts] * 6).astype(jnp.float32)
    pieces = list(pack(member_ref, queries, out_grad, bounds))
    exchange = [
        [(c, c ^ d) for c in range(column_count)] for d in range(BLOCK)
    ]
    for d in EARLY + LATE:
        pieces[d] = lax.ppermute(pieces[d], "ctx", exchange[d])

    recv_label = received[:, 2 * head_width].astype(jnp.int32)
    filling = recv_label[:, None] - 1 == token_index[None, :]
    filling_half = filling.astype(half)
    memory = jnp.dot(
        filling_half.T, received[:, : 2 * head_width], preferred_element_type=jnp.float32
    ).astype(half)
    by_member = memory.reshape(enc_rows, 2, BLOCK, part_width // 2).transpose(2, 0, 1, 3)
    by_member = by_member.reshape(1, BLOCK, enc_rows, part_width)
    by_column = jnp.broadcast_to(
        by_member, (column_count // BLOCK, BLOCK, enc_rows, part_width)
    ).reshape(column_count, enc_rows, part_width)
    for d in EARLY:
        by_column, pieces[d] = lax.optimization_barrier((by_column, pieces[d]))
    group_part = lax.all_to_all(by_column, "ctx", split_axis=0, concat_axis=0, tiled=True)
    group_part = group_part.reshape(column_count * enc_rows, part_width)

    part_grad, *results = attend(member_ref, far, spans, group_part, pieces)

    for d in RETURNED + LAST:
        results[d] = lax.ppermute(results[d], "ctx", exchange[d])
    part_grad = part_grad.reshape(column_count, enc_rows, part_width)
    partials = lax.all_to_all(part_grad, "ctx", split_axis=0, concat_axis=0, tiled=True)
    for d in RETURNED:
        partials, results[d] = lax.optimization_barrier((partials, results[d]))
    partials = partials.reshape(column_count // BLOCK, BLOCK, enc_rows, 2, part_width // 2)
    memory_grad = jnp.sum(partials.astype(jnp.float32), axis=0).astype(half)
    memory_grad = memory_grad.transpose(1, 2, 0, 3).reshape(enc_rows, 2 * head_width)
    back_pairs = jnp.dot(filling_half, memory_grad, preferred_element_type=jnp.float32).astype(half)
    returned = lax.all_to_all(back_pairs, "dp", split_axis=0, concat_axis=0, tiled=True)
    enc_grads = jnp.dot(placing_half.T, returned, preferred_element_type=jnp.float32).astype(half)

    attended, query_grad = unpack(member_ref, results, head_width)
    return attended, query_grad, enc_grads.reshape(enc_rows, 2, head_width)


def solution(mesh):
    return jax.shard_map(
        shards,
        mesh=mesh,
        in_specs=(
            P(("dp", "ctx"), None),
            P(("dp", "ctx"), None, None),
            P(("dp", "ctx"), None),
            P(("dp", "ctx")),
            P("dp", None),
            P("dp", "ctx"),
        ),
        out_specs=(P(("dp", "ctx"), None), P(("dp", "ctx"), None), P(("dp", "ctx"), None, None)),
        check_vma=False,
    )
```

```python
import math

import jax
import jax.numpy as jnp
from jax import lax
from jax.experimental import pallas as pl
from jax.experimental.pallas import tpu as pltpu
from jax.sharding import PartitionSpec as P

DH = 64
LANES = 128
TILE = 16
FAR = -1e30
BLOCK = 8
CHUNK = 256
SPANS = (64, 128, 192, 256, 384, 512)
TOGETHER = (192,)
VMEM_BYTES = 48 * 1024 * 1024
COPY_BYTES = 16 * 1024 * 1024
EARLY, LATE = (2, 6, 5, 4), (7, 3, 1)
RETURNED, LAST = (2, 1, 3), (6, 7, 5, 4)
VMEM = pl.BlockSpec(memory_space=pltpu.VMEM)
ANY = pl.BlockSpec(memory_space=pl.ANY)
SMEM = pl.BlockSpec(memory_space=pltpu.SMEM)


def run_copies(copies):
    for copy in copies:
        copy.start()
    for copy in copies:
        copy.wait()


def pack_kernel(member_ref, queries_ref, grads_ref, bounds_ref, *pieces):
    half = queries_ref.shape[1] // len(pieces)
    rows = queries_ref.shape[0]
    for d, piece in enumerate(pieces):
        columns = pl.ds(pl.multiple_of((member_ref[0] ^ d) * half, half), half)
        piece[pl.ds(0, rows), pl.ds(0, half)] = queries_ref[:, columns]
        piece[pl.ds(0, rows), pl.ds(half, half)] = grads_ref[:, columns]
        piece[pl.ds(rows, TILE), :] = bounds_ref[...]


def pack(member, queries, grads, bounds):
    rows, width = queries.shape
    piece = jax.ShapeDtypeStruct((rows + TILE, 2 * width // BLOCK), queries.dtype)
    return pl.pallas_call(
        pack_kernel,
        out_shape=[piece] * BLOCK,
        in_specs=[SMEM, VMEM, VMEM, VMEM],
        out_specs=[VMEM] * BLOCK,
        compiler_params=pltpu.CompilerParams(vmem_limit_bytes=COPY_BYTES),
        cost_estimate=pl.CostEstimate(
            flops=0, bytes_accessed=4 * 2 * rows * width, transcendentals=0
        ),
        name="pack",
    )(member, queries, grads, bounds)


def unpack_kernel(member_ref, *rest):
    pieces, (attended_ref, query_grad_ref) = rest[:-2], rest[-2:]
    half = attended_ref.shape[1] // len(pieces)
    for d, piece in enumerate(pieces):
        columns = pl.ds(pl.multiple_of((member_ref[0] ^ d) * half, half), half)
        attended_ref[:, columns] = piece[:, pl.ds(0, half)]
        query_grad_ref[:, columns] = piece[:, pl.ds(half, half)]


def unpack(member, pieces, width):
    rows = pieces[0].shape[0]
    out = jax.ShapeDtypeStruct((rows, width), pieces[0].dtype)
    return pl.pallas_call(
        unpack_kernel,
        out_shape=[out, out],
        in_specs=[SMEM] + [VMEM] * BLOCK,
        out_specs=[VMEM, VMEM],
        compiler_params=pltpu.CompilerParams(vmem_limit_bytes=COPY_BYTES),
        cost_estimate=pl.CostEstimate(
            flops=0, bytes_accessed=4 * 2 * rows * width, transcendentals=0
        ),
        name="unpack",
    )(member, *pieces)


def nt_dot(left, right):
    return lax.dot_general(
        left, right, (((1,), (1,)), ((), ())), preferred_element_type=jnp.float32
    )


def tn_dot(left, right):
    return lax.dot_general(
        left, right, (((0,), (0,)), ((), ())), preferred_element_type=jnp.float32
    )


def nn_dot(left, right):
    return jnp.dot(left, right, preferred_element_type=jnp.float32)


def attend_kernel(member_ref, far_ref, spans_ref, kv_ref, *rest):
    pieces, rest = rest[:BLOCK], rest[BLOCK:]
    grad_ref, outs, rest = rest[0], rest[1 : 1 + BLOCK], rest[1 + BLOCK :]
    held, edges, spread, docs, keys, key_aug, values, key_acc, value_acc, result, window, sems = rest
    rows = pieces[0].shape[0] - TILE
    mem_rows, width = kv_ref.shape
    half = width // 2
    pairs = half // LANES
    chunks = BLOCK * rows // CHUNK
    scale = 1.0 / math.sqrt(DH)

    def place(d):
        return pl.ds(pl.multiple_of((member_ref[0] ^ d) * rows, rows), rows)

    loads = []
    for d, piece in enumerate(pieces):
        loads += [
            pltpu.make_async_copy(piece.at[pl.ds(0, rows)], held.at[place(d)], sems.at[0, d]),
            pltpu.make_async_copy(
                piece.at[pl.ds(rows, TILE), pl.ds(0, LANES)],
                edges.at[member_ref[0] ^ d],
                sems.at[1, d],
            ),
        ]
    for load in loads:
        load.start()
    low = lax.broadcasted_iota(jnp.int32, (mem_rows, LANES), 1) < DH
    zero = jnp.zeros((mem_rows, LANES), jnp.bfloat16)
    for pair in range(pairs):
        key_pair = kv_ref[:, pl.ds(pair * LANES, LANES)] * jnp.bfloat16(scale)
        value_pair = kv_ref[:, pl.ds(half + pair * LANES, LANES)]
        keys[pair] = key_pair
        for head in range(2):
            mine = low if head == 0 else ~low
            key_aug[pair, head, :, pl.ds(0, LANES)] = jnp.where(mine, key_pair, zero)
            key_aug[pair, head, :, pl.ds(LANES, LANES)] = far_ref[...]
            values[pair, head] = jnp.where(mine, value_pair, zero)
    key_acc[...] = jnp.zeros_like(key_acc)
    value_acc[...] = jnp.zeros_like(value_acc)

    for load in loads:
        load.wait()
    row = lax.broadcasted_iota(jnp.int32, (rows, LANES), 0).astype(jnp.float32)
    for source in range(BLOCK):
        edge = edges[source].astype(jnp.float32)
        first, last = edge[0:1], edge[1:2]
        inside = (row >= first) & (row < last)
        docs[pl.ds(source * rows, rows), :] = jnp.where(inside, 1.0, 0.0).astype(jnp.bfloat16)
        spread[0, pl.ds(source, 1), :] = first + source * rows
        spread[1, pl.ds(source, 1), :] = last + source * rows
    for chunk in range(chunks):
        opens = jnp.maximum(spread[0], float(chunk * CHUNK))
        present = opens < jnp.minimum(spread[1], float((chunk + 1) * CHUNK))
        window[chunk, 0] = jnp.min(jnp.where(present, spans_ref[0:1], float(mem_rows))).astype(
            jnp.int32
        )
        window[chunk, 1] = jnp.max(jnp.where(present, spans_ref[1:2], 0.0)).astype(jnp.int32)

    key_columns = [pl.ds(pair * LANES, LANES) for pair in range(pairs)]
    value_columns = [pl.ds(half + pair * LANES, LANES) for pair in range(pairs)]

    def on_windows(heres, starts, span):
        half_lanes = lax.broadcasted_iota(jnp.int32, (span, LANES), 1) < DH
        items = [
            (pair, here, pl.ds(start, span))
            for here, start in zip(heres, starts)
            for pair in range(pairs)
        ]
        query = [held[here, key_columns[pair]] for pair, here, _ in items]
        grad = [held[here, value_columns[pair]] for pair, here, _ in items]
        scores = [
            nt_dot(
                key_aug[pair, :, mine, :].reshape(2 * span, 2 * LANES),
                jnp.concatenate([query[i], docs[here, :]], axis=1),
            ).reshape(2, span, CHUNK)
            for i, (pair, here, mine) in enumerate(items)
        ]
        grad_normed = [
            nt_dot(values[pair, :, mine, :].reshape(2 * span, LANES), grad[i]).reshape(
                2, span, CHUNK
            )
            for i, (pair, here, mine) in enumerate(items)
        ]
        rounded, grad_scores = [], []
        for i in range(len(items)):
            top = jnp.max(scores[i], axis=1, keepdims=True)
            weights = jnp.exp(scores[i] - top)
            normed = weights * (1.0 / jnp.sum(weights, axis=1, keepdims=True))
            delta = jnp.sum(normed * grad_normed[i], axis=1, keepdims=True)
            rounded.append(normed.astype(jnp.bfloat16))
            grad_scores.append((normed * (grad_normed[i] - delta)).astype(jnp.bfloat16))
        for i, (pair, here, mine) in enumerate(items):
            key_grad = nn_dot(grad_scores[i].reshape(2 * span, CHUNK), query[i])
            value_grad = nn_dot(rounded[i].reshape(2 * span, CHUNK), grad[i])
            key_acc[pair, mine, :] += jnp.where(half_lanes, key_grad[:span], key_grad[span:])
            value_acc[pair, mine, :] += jnp.where(half_lanes, value_grad[:span], value_grad[span:])
        for i, (pair, here, mine) in enumerate(items):
            key_turned = keys[pair, mine, :].T
            value_turned = kv_ref[mine, value_columns[pair]].T
            for columns, turned, terms in (
                (key_columns[pair], value_turned, rounded[i]),
                (value_columns[pair], key_turned, grad_scores[i]),
            ):
                both = [
                    nn_dot(turned[head * DH : (head + 1) * DH], terms[head]) for head in range(2)
                ]
                result[here, columns] = jnp.concatenate(both, axis=0).astype(jnp.bfloat16).T

    def start_of(chunk, span):
        first = jnp.minimum((window[chunk, 0] // 16) * 16, mem_rows - span)
        return pl.multiple_of(first, 16)

    def fits(chunk, span):
        return window[chunk, 1] <= start_of(chunk, span) + span

    def step(chunk, carry):
        here = pl.ds(pl.multiple_of(chunk * CHUNK, CHUNK), CHUNK)
        taken = jnp.bool_(False)
        for span in SPANS:
            fit = fits(chunk, span)

            @pl.when(fit & ~taken)
            def _(span=span):
                on_windows([here], [start_of(chunk, span)], span)

            taken = taken | fit
        return carry

    taken = jnp.bool_(False)
    for span in TOGETHER:
        fit = jnp.bool_(True)
        for chunk in range(chunks):
            fit = fit & fits(chunk, span)

        @pl.when(fit & ~taken)
        def _(span=span):
            on_windows(
                [pl.ds(chunk * CHUNK, CHUNK) for chunk in range(chunks)],
                [start_of(chunk, span) for chunk in range(chunks)],
                span,
            )

        taken = taken | fit

    @pl.when(~taken)
    def _():
        lax.fori_loop(0, chunks, step, 0)

    for pair in range(pairs):
        grad_ref[:, pl.ds(pair * LANES, LANES)] = (key_acc[pair] * scale).astype(jnp.bfloat16)
        grad_ref[:, pl.ds(half + pair * LANES, LANES)] = value_acc[pair].astype(jnp.bfloat16)
    run_copies(
        [
            pltpu.make_async_copy(result.at[place(d)], out, sems.at[0, d])
            for d, out in enumerate(outs)
        ]
    )


def attend(member, far, spans, memory, pieces):
    rows = pieces[0].shape[0] - TILE
    mem_rows, width = memory.shape
    all_rows = BLOCK * rows
    heads = width // (2 * DH)
    half = jnp.bfloat16
    return pl.pallas_call(
        attend_kernel,
        out_shape=[jax.ShapeDtypeStruct((mem_rows, width), half)]
        + [jax.ShapeDtypeStruct((rows, width), half)] * BLOCK,
        in_specs=[SMEM] + [VMEM] * 3 + [ANY] * BLOCK,
        out_specs=[VMEM] + [ANY] * BLOCK,
        scratch_shapes=[
            pltpu.VMEM((all_rows, width), half),
            pltpu.VMEM((BLOCK, TILE, LANES), half),
            pltpu.VMEM((2, BLOCK, LANES), jnp.float32),
            pltpu.VMEM((all_rows, LANES), half),
            pltpu.VMEM((heads // 2, mem_rows, LANES), half),
            pltpu.VMEM((heads // 2, 2, mem_rows, 2 * LANES), half),
            pltpu.VMEM((heads // 2, 2, mem_rows, LANES), half),
            pltpu.VMEM((heads // 2, mem_rows, LANES), jnp.float32),
            pltpu.VMEM((heads // 2, mem_rows, LANES), jnp.float32),
            pltpu.VMEM((all_rows, width), half),
            pltpu.SMEM((8, 2), jnp.int32),
            pltpu.SemaphoreType.DMA((2, BLOCK)),
        ],
        compiler_params=pltpu.CompilerParams(vmem_limit_bytes=VMEM_BYTES),
        cost_estimate=pl.CostEstimate(
            flops=6 * 2 * all_rows * mem_rows * width // 2,
            bytes_accessed=8 * all_rows * width,
            transcendentals=all_rows * mem_rows * width // (2 * DH),
        ),
        name="attend",
    )(member, far, spans, memory, *pieces)


def shards(queries, key_value, out_grad, packing, memory_docs, decoder_docs):
    group_count = lax.axis_size("dp")
    column_count = lax.axis_size("ctx")
    enc_rows, _, head_width = key_value.shape
    part_width = 2 * head_width // BLOCK
    slot_cap = 2
    slot_count = group_count * slot_cap
    half = jnp.bfloat16

    target_group = packing // enc_rows
    token_index = jnp.arange(enc_rows, dtype=jnp.int32)
    earlier = (target_group[:, None] == target_group[None, :]) & (
        token_index[None, :] < token_index[:, None]
    )
    send_slot = target_group * slot_cap + jnp.sum(earlier, axis=1)
    placing = jnp.arange(slot_count, dtype=jnp.int32)[:, None] == send_slot[None, :]
    placing_half = placing.astype(half)
    labels = jnp.broadcast_to(
        (packing % enc_rows + 1).astype(half)[:, None], (enc_rows, LANES)
    )
    flat_pairs = jnp.concatenate([key_value.reshape(enc_rows, 2 * head_width), labels], axis=1)
    send_pairs = jnp.dot(placing_half, flat_pairs, preferred_element_type=jnp.float32).astype(half)
    received = lax.all_to_all(send_pairs, "dp", split_axis=0, concat_axis=0, tiled=True)

    member = lax.axis_index("ctx") % BLOCK
    member_ref = member.reshape(1).astype(jnp.int32)
    doc_lanes = jnp.arange(LANES, dtype=jnp.int32)
    bounds = jnp.stack(
        [
            jnp.sum(decoder_docs[0][:, None] < doc_lanes[None, :], axis=0),
            jnp.sum(decoder_docs[0][:, None] <= doc_lanes[None, :], axis=0),
        ]
    ).astype(half)
    bounds = jnp.pad(bounds, ((0, TILE - 2), (0, part_width - LANES)))
    far = jnp.where(memory_docs[0][:, None] == doc_lanes[None, :], 0.0, FAR).astype(half)
    starts = jnp.sum(memory_docs[0][:, None] < doc_lanes[None, :], axis=0)
    ends = jnp.sum(memory_docs[0][:, None] <= doc_lanes[None, :], axis=0)
    spans = jnp.stack([starts, ends] + [starts] * 6).astype(jnp.float32)
    pieces = list(pack(member_ref, queries, out_grad, bounds))
    exchange = [
        [(c, c ^ d) for c in range(column_count)] for d in range(BLOCK)
    ]
    for d in EARLY + LATE:
        pieces[d] = lax.ppermute(pieces[d], "ctx", exchange[d])

    recv_label = received[:, 2 * head_width].astype(jnp.int32)
    filling = recv_label[:, None] - 1 == token_index[None, :]
    filling_half = filling.astype(half)
    memory = jnp.dot(
        filling_half.T, received[:, : 2 * head_width], preferred_element_type=jnp.float32
    ).astype(half)
    by_member = memory.reshape(enc_rows, 2, BLOCK, part_width // 2).transpose(2, 0, 1, 3)
    by_member = by_member.reshape(1, BLOCK, enc_rows, part_width)
    by_column = jnp.broadcast_to(
        by_member, (column_count // BLOCK, BLOCK, enc_rows, part_width)
    ).reshape(column_count, enc_rows, part_width)
    for d in EARLY:
        by_column, pieces[d] = lax.optimization_barrier((by_column, pieces[d]))
    group_part = lax.all_to_all(by_column, "ctx", split_axis=0, concat_axis=0, tiled=True)
    group_part = group_part.reshape(column_count * enc_rows, part_width)

    part_grad, *results = attend(member_ref, far, spans, group_part, pieces)

    for d in RETURNED + LAST:
        results[d] = lax.ppermute(results[d], "ctx", exchange[d])
    part_grad = part_grad.reshape(column_count, enc_rows, part_width)
    partials = lax.all_to_all(part_grad, "ctx", split_axis=0, concat_axis=0, tiled=True)
    for d in RETURNED:
        partials, results[d] = lax.optimization_barrier((partials, results[d]))
    partials = partials.reshape(column_count // BLOCK, BLOCK, enc_rows, 2, part_width // 2)
    memory_grad = jnp.sum(partials.astype(jnp.float32), axis=0).astype(half)
    memory_grad = memory_grad.transpose(1, 2, 0, 3).reshape(enc_rows, 2 * head_width)
    back_pairs = jnp.dot(filling_half, memory_grad, preferred_element_type=jnp.float32).astype(half)
    returned = lax.all_to_all(back_pairs, "dp", split_axis=0, concat_axis=0, tiled=True)
    enc_grads = jnp.dot(placing_half.T, returned, preferred_element_type=jnp.float32).astype(half)

    attended, query_grad = unpack(member_ref, results, head_width)
    return attended, query_grad, enc_grads.reshape(enc_rows, 2, head_width)


def solution(mesh):
    return jax.shard_map(
        shards,
        mesh=mesh,
        in_specs=(
            P(("dp", "ctx"), None),
            P(("dp", "ctx"), None, None),
            P(("dp", "ctx"), None),
            P(("dp", "ctx")),
            P("dp", None),
            P("dp", "ctx"),
        ),
        out_specs=(P(("dp", "ctx"), None), P(("dp", "ctx"), None), P(("dp", "ctx"), None, None)),
        check_vma=False,
    )
```

```python
import math

import jax
import jax.numpy as jnp
from jax import lax
from jax.experimental import pallas as pl
from jax.experimental.pallas import tpu as pltpu
from jax.sharding import PartitionSpec as P

DH = 64
LANES = 128
TILE = 16
FAR = -1e30
BLOCK = 8
CHUNK = 256
SPANS = (64, 128, 192, 256, 384, 512)
TOGETHER = (192,)
VMEM_BYTES = 48 * 1024 * 1024
COPY_BYTES = 16 * 1024 * 1024
EARLY, LATE = (2, 6, 5, 7), (4, 3, 1)
RETURNED, LAST = (2, 1, 3, 4), (6, 7, 5)
VMEM = pl.BlockSpec(memory_space=pltpu.VMEM)
ANY = pl.BlockSpec(memory_space=pl.ANY)
SMEM = pl.BlockSpec(memory_space=pltpu.SMEM)


def run_copies(copies):
    for copy in copies:
        copy.start()
    for copy in copies:
        copy.wait()


def pack_kernel(member_ref, queries_ref, grads_ref, bounds_ref, *pieces):
    half = queries_ref.shape[1] // len(pieces)
    rows = queries_ref.shape[0]
    for d, piece in enumerate(pieces):
        columns = pl.ds(pl.multiple_of((member_ref[0] ^ d) * half, half), half)
        piece[pl.ds(0, rows), pl.ds(0, half)] = queries_ref[:, columns]
        piece[pl.ds(0, rows), pl.ds(half, half)] = grads_ref[:, columns]
        piece[pl.ds(rows, TILE), :] = bounds_ref[...]


def pack(member, queries, grads, bounds):
    rows, width = queries.shape
    piece = jax.ShapeDtypeStruct((rows + TILE, 2 * width // BLOCK), queries.dtype)
    return pl.pallas_call(
        pack_kernel,
        out_shape=[piece] * BLOCK,
        in_specs=[SMEM, VMEM, VMEM, VMEM],
        out_specs=[VMEM] * BLOCK,
        compiler_params=pltpu.CompilerParams(vmem_limit_bytes=COPY_BYTES),
        cost_estimate=pl.CostEstimate(
            flops=0, bytes_accessed=4 * 2 * rows * width, transcendentals=0
        ),
        name="pack",
    )(member, queries, grads, bounds)


def unpack_kernel(member_ref, *rest):
    pieces, (attended_ref, query_grad_ref) = rest[:-2], rest[-2:]
    half = attended_ref.shape[1] // len(pieces)
    for d, piece in enumerate(pieces):
        columns = pl.ds(pl.multiple_of((member_ref[0] ^ d) * half, half), half)
        attended_ref[:, columns] = piece[:, pl.ds(0, half)]
        query_grad_ref[:, columns] = piece[:, pl.ds(half, half)]


def unpack(member, pieces, width):
    rows = pieces[0].shape[0]
    out = jax.ShapeDtypeStruct((rows, width), pieces[0].dtype)
    return pl.pallas_call(
        unpack_kernel,
        out_shape=[out, out],
        in_specs=[SMEM] + [VMEM] * BLOCK,
        out_specs=[VMEM, VMEM],
        compiler_params=pltpu.CompilerParams(vmem_limit_bytes=COPY_BYTES),
        cost_estimate=pl.CostEstimate(
            flops=0, bytes_accessed=4 * 2 * rows * width, transcendentals=0
        ),
        name="unpack",
    )(member, *pieces)


def nt_dot(left, right):
    return lax.dot_general(
        left, right, (((1,), (1,)), ((), ())), preferred_element_type=jnp.float32
    )


def tn_dot(left, right):
    return lax.dot_general(
        left, right, (((0,), (0,)), ((), ())), preferred_element_type=jnp.float32
    )


def nn_dot(left, right):
    return jnp.dot(left, right, preferred_element_type=jnp.float32)


def attend_kernel(member_ref, far_ref, spans_ref, kv_ref, *rest):
    pieces, rest = rest[:BLOCK], rest[BLOCK:]
    grad_ref, outs, rest = rest[0], rest[1 : 1 + BLOCK], rest[1 + BLOCK :]
    held, edges, spread, docs, keys, key_aug, values, key_acc, value_acc, result, window, sems = rest
    rows = pieces[0].shape[0] - TILE
    mem_rows, width = kv_ref.shape
    half = width // 2
    pairs = half // LANES
    chunks = BLOCK * rows // CHUNK
    scale = 1.0 / math.sqrt(DH)

    def place(d):
        return pl.ds(pl.multiple_of((member_ref[0] ^ d) * rows, rows), rows)

    loads = []
    for d, piece in enumerate(pieces):
        loads += [
            pltpu.make_async_copy(piece.at[pl.ds(0, rows)], held.at[place(d)], sems.at[0, d]),
            pltpu.make_async_copy(
                piece.at[pl.ds(rows, TILE), pl.ds(0, LANES)],
                edges.at[member_ref[0] ^ d],
                sems.at[1, d],
            ),
        ]
    for load in loads:
        load.start()
    low = lax.broadcasted_iota(jnp.int32, (mem_rows, LANES), 1) < DH
    zero = jnp.zeros((mem_rows, LANES), jnp.bfloat16)
    for pair in range(pairs):
        key_pair = kv_ref[:, pl.ds(pair * LANES, LANES)] * jnp.bfloat16(scale)
        value_pair = kv_ref[:, pl.ds(half + pair * LANES, LANES)]
        keys[pair] = key_pair
        for head in range(2):
            mine = low if head == 0 else ~low
            key_aug[pair, head, :, pl.ds(0, LANES)] = jnp.where(mine, key_pair, zero)
            key_aug[pair, head, :, pl.ds(LANES, LANES)] = far_ref[...]
            values[pair, head] = jnp.where(mine, value_pair, zero)
    key_acc[...] = jnp.zeros_like(key_acc)
    value_acc[...] = jnp.zeros_like(value_acc)

    for load in loads:
        load.wait()
    row = lax.broadcasted_iota(jnp.int32, (rows, LANES), 0).astype(jnp.float32)
    for source in range(BLOCK):
        edge = edges[source].astype(jnp.float32)
        first, last = edge[0:1], edge[1:2]
        inside = (row >= first) & (row < last)
        docs[pl.ds(source * rows, rows), :] = jnp.where(inside, 1.0, 0.0).astype(jnp.bfloat16)
        spread[0, pl.ds(source, 1), :] = first + source * rows
        spread[1, pl.ds(source, 1), :] = last + source * rows
    for chunk in range(chunks):
        opens = jnp.maximum(spread[0], float(chunk * CHUNK))
        present = opens < jnp.minimum(spread[1], float((chunk + 1) * CHUNK))
        window[chunk, 0] = jnp.min(jnp.where(present, spans_ref[0:1], float(mem_rows))).astype(
            jnp.int32
        )
        window[chunk, 1] = jnp.max(jnp.where(present, spans_ref[1:2], 0.0)).astype(jnp.int32)

    key_columns = [pl.ds(pair * LANES, LANES) for pair in range(pairs)]
    value_columns = [pl.ds(half + pair * LANES, LANES) for pair in range(pairs)]

    def on_windows(heres, starts, span):
        half_lanes = lax.broadcasted_iota(jnp.int32, (span, LANES), 1) < DH
        items = [
            (pair, here, pl.ds(start, span))
            for here, start in zip(heres, starts)
            for pair in range(pairs)
        ]
        query = [held[here, key_columns[pair]] for pair, here, _ in items]
        grad = [held[here, value_columns[pair]] for pair, here, _ in items]
        scores = [
            nt_dot(
                key_aug[pair, :, mine, :].reshape(2 * span, 2 * LANES),
                jnp.concatenate([query[i], docs[here, :]], axis=1),
            ).reshape(2, span, CHUNK)
            for i, (pair, here, mine) in enumerate(items)
        ]
        grad_normed = [
            nt_dot(values[pair, :, mine, :].reshape(2 * span, LANES), grad[i]).reshape(
                2, span, CHUNK
            )
            for i, (pair, here, mine) in enumerate(items)
        ]
        rounded, grad_scores = [], []
        for i in range(len(items)):
            top = jnp.max(scores[i], axis=1, keepdims=True)
            weights = jnp.exp(scores[i] - top)
            normed = weights * (1.0 / jnp.sum(weights, axis=1, keepdims=True))
            delta = jnp.sum(normed * grad_normed[i], axis=1, keepdims=True)
            rounded.append(normed.astype(jnp.bfloat16))
            grad_scores.append((normed * (grad_normed[i] - delta)).astype(jnp.bfloat16))
        for i, (pair, here, mine) in enumerate(items):
            key_grad = nn_dot(grad_scores[i].reshape(2 * span, CHUNK), query[i])
            value_grad = nn_dot(rounded[i].reshape(2 * span, CHUNK), grad[i])
            key_acc[pair, mine, :] += jnp.where(half_lanes, key_grad[:span], key_grad[span:])
            value_acc[pair, mine, :] += jnp.where(half_lanes, value_grad[:span], value_grad[span:])
        for i, (pair, here, mine) in enumerate(items):
            key_turned = keys[pair, mine, :].T
            value_turned = kv_ref[mine, value_columns[pair]].T
            for columns, turned, terms in (
                (key_columns[pair], value_turned, rounded[i]),
                (value_columns[pair], key_turned, grad_scores[i]),
            ):
                both = [
                    nn_dot(turned[head * DH : (head + 1) * DH], terms[head]) for head in range(2)
                ]
                result[here, columns] = jnp.concatenate(both, axis=0).astype(jnp.bfloat16).T

    def start_of(chunk, span):
        first = jnp.minimum((window[chunk, 0] // 16) * 16, mem_rows - span)
        return pl.multiple_of(first, 16)

    def fits(chunk, span):
        return window[chunk, 1] <= start_of(chunk, span) + span

    def step(chunk, carry):
        here = pl.ds(pl.multiple_of(chunk * CHUNK, CHUNK), CHUNK)
        taken = jnp.bool_(False)
        for span in SPANS:
            fit = fits(chunk, span)

            @pl.when(fit & ~taken)
            def _(span=span):
                on_windows([here], [start_of(chunk, span)], span)

            taken = taken | fit
        return carry

    taken = jnp.bool_(False)
    for span in TOGETHER:
        fit = jnp.bool_(True)
        for chunk in range(chunks):
            fit = fit & fits(chunk, span)

        @pl.when(fit & ~taken)
        def _(span=span):
            on_windows(
                [pl.ds(chunk * CHUNK, CHUNK) for chunk in range(chunks)],
                [start_of(chunk, span) for chunk in range(chunks)],
                span,
            )

        taken = taken | fit

    @pl.when(~taken)
    def _():
        lax.fori_loop(0, chunks, step, 0)

    for pair in range(pairs):
        grad_ref[:, pl.ds(pair * LANES, LANES)] = (key_acc[pair] * scale).astype(jnp.bfloat16)
        grad_ref[:, pl.ds(half + pair * LANES, LANES)] = value_acc[pair].astype(jnp.bfloat16)
    run_copies(
        [
            pltpu.make_async_copy(result.at[place(d)], out, sems.at[0, d])
            for d, out in enumerate(outs)
        ]
    )


def attend(member, far, spans, memory, pieces):
    rows = pieces[0].shape[0] - TILE
    mem_rows, width = memory.shape
    all_rows = BLOCK * rows
    heads = width // (2 * DH)
    half = jnp.bfloat16
    return pl.pallas_call(
        attend_kernel,
        out_shape=[jax.ShapeDtypeStruct((mem_rows, width), half)]
        + [jax.ShapeDtypeStruct((rows, width), half)] * BLOCK,
        in_specs=[SMEM] + [VMEM] * 3 + [ANY] * BLOCK,
        out_specs=[VMEM] + [ANY] * BLOCK,
        scratch_shapes=[
            pltpu.VMEM((all_rows, width), half),
            pltpu.VMEM((BLOCK, TILE, LANES), half),
            pltpu.VMEM((2, BLOCK, LANES), jnp.float32),
            pltpu.VMEM((all_rows, LANES), half),
            pltpu.VMEM((heads // 2, mem_rows, LANES), half),
            pltpu.VMEM((heads // 2, 2, mem_rows, 2 * LANES), half),
            pltpu.VMEM((heads // 2, 2, mem_rows, LANES), half),
            pltpu.VMEM((heads // 2, mem_rows, LANES), jnp.float32),
            pltpu.VMEM((heads // 2, mem_rows, LANES), jnp.float32),
            pltpu.VMEM((all_rows, width), half),
            pltpu.SMEM((8, 2), jnp.int32),
            pltpu.SemaphoreType.DMA((2, BLOCK)),
        ],
        compiler_params=pltpu.CompilerParams(vmem_limit_bytes=VMEM_BYTES),
        cost_estimate=pl.CostEstimate(
            flops=6 * 2 * all_rows * mem_rows * width // 2,
            bytes_accessed=8 * all_rows * width,
            transcendentals=all_rows * mem_rows * width // (2 * DH),
        ),
        name="attend",
    )(member, far, spans, memory, *pieces)


def shards(queries, key_value, out_grad, packing, memory_docs, decoder_docs):
    group_count = lax.axis_size("dp")
    column_count = lax.axis_size("ctx")
    enc_rows, _, head_width = key_value.shape
    part_width = 2 * head_width // BLOCK
    slot_cap = 2
    slot_count = group_count * slot_cap
    half = jnp.bfloat16

    target_group = packing // enc_rows
    token_index = jnp.arange(enc_rows, dtype=jnp.int32)
    earlier = (target_group[:, None] == target_group[None, :]) & (
        token_index[None, :] < token_index[:, None]
    )
    send_slot = target_group * slot_cap + jnp.sum(earlier, axis=1)
    placing = jnp.arange(slot_count, dtype=jnp.int32)[:, None] == send_slot[None, :]
    placing_half = placing.astype(half)
    labels = jnp.broadcast_to(
        (packing % enc_rows + 1).astype(half)[:, None], (enc_rows, LANES)
    )
    flat_pairs = jnp.concatenate([key_value.reshape(enc_rows, 2 * head_width), labels], axis=1)
    send_pairs = jnp.dot(placing_half, flat_pairs, preferred_element_type=jnp.float32).astype(half)
    received = lax.all_to_all(send_pairs, "dp", split_axis=0, concat_axis=0, tiled=True)

    member = lax.axis_index("ctx") % BLOCK
    member_ref = member.reshape(1).astype(jnp.int32)
    doc_lanes = jnp.arange(LANES, dtype=jnp.int32)
    bounds = jnp.stack(
        [
            jnp.sum(decoder_docs[0][:, None] < doc_lanes[None, :], axis=0),
            jnp.sum(decoder_docs[0][:, None] <= doc_lanes[None, :], axis=0),
        ]
    ).astype(half)
    bounds = jnp.pad(bounds, ((0, TILE - 2), (0, part_width - LANES)))
    far = jnp.where(memory_docs[0][:, None] == doc_lanes[None, :], 0.0, FAR).astype(half)
    starts = jnp.sum(memory_docs[0][:, None] < doc_lanes[None, :], axis=0)
    ends = jnp.sum(memory_docs[0][:, None] <= doc_lanes[None, :], axis=0)
    spans = jnp.stack([starts, ends] + [starts] * 6).astype(jnp.float32)
    pieces = list(pack(member_ref, queries, out_grad, bounds))
    exchange = [
        [(c, c ^ d) for c in range(column_count)] for d in range(BLOCK)
    ]
    for d in EARLY + LATE:
        pieces[d] = lax.ppermute(pieces[d], "ctx", exchange[d])

    recv_label = received[:, 2 * head_width].astype(jnp.int32)
    filling = recv_label[:, None] - 1 == token_index[None, :]
    filling_half = filling.astype(half)
    memory = jnp.dot(
        filling_half.T, received[:, : 2 * head_width], preferred_element_type=jnp.float32
    ).astype(half)
    by_member = memory.reshape(enc_rows, 2, BLOCK, part_width // 2).transpose(2, 0, 1, 3)
    by_member = by_member.reshape(1, BLOCK, enc_rows, part_width)
    by_column = jnp.broadcast_to(
        by_member, (column_count // BLOCK, BLOCK, enc_rows, part_width)
    ).reshape(column_count, enc_rows, part_width)
    for d in EARLY:
        by_column, pieces[d] = lax.optimization_barrier((by_column, pieces[d]))
    group_part = lax.all_to_all(by_column, "ctx", split_axis=0, concat_axis=0, tiled=True)
    group_part = group_part.reshape(column_count * enc_rows, part_width)

    part_grad, *results = attend(member_ref, far, spans, group_part, pieces)

    for d in RETURNED + LAST:
        results[d] = lax.ppermute(results[d], "ctx", exchange[d])
    part_grad = part_grad.reshape(column_count, enc_rows, part_width)
    partials = lax.all_to_all(part_grad, "ctx", split_axis=0, concat_axis=0, tiled=True)
    for d in RETURNED:
        partials, results[d] = lax.optimization_barrier((partials, results[d]))
    partials = partials.reshape(column_count // BLOCK, BLOCK, enc_rows, 2, part_width // 2)
    memory_grad = jnp.sum(partials.astype(jnp.float32), axis=0).astype(half)
    memory_grad = memory_grad.transpose(1, 2, 0, 3).reshape(enc_rows, 2 * head_width)
    back_pairs = jnp.dot(filling_half, memory_grad, preferred_element_type=jnp.float32).astype(half)
    returned = lax.all_to_all(back_pairs, "dp", split_axis=0, concat_axis=0, tiled=True)
    enc_grads = jnp.dot(placing_half.T, returned, preferred_element_type=jnp.float32).astype(half)

    attended, query_grad = unpack(member_ref, results, head_width)
    return attended, query_grad, enc_grads.reshape(enc_rows, 2, head_width)


def solution(mesh):
    return jax.shard_map(
        shards,
        mesh=mesh,
        in_specs=(
            P(("dp", "ctx"), None),
            P(("dp", "ctx"), None, None),
            P(("dp", "ctx"), None),
            P(("dp", "ctx")),
            P("dp", None),
            P("dp", "ctx"),
        ),
        out_specs=(P(("dp", "ctx"), None), P(("dp", "ctx"), None), P(("dp", "ctx"), None, None)),
        check_vma=False,
    )
```
